32 devices in a mesh: grp: 4 (over x, core), exp: 8 (over z, y).
Axes of the slice: x: 2, y: 2, z: 4, core: 2. Of those that a mesh axis runs over, the one named last changes fastest.
Arguments:
- tokens: bfloat16 [4096, 4096], P(('grp', 'exp')), may hold values from -6 to 6
- expert_ids: int32 [4096, 8], P(('grp', 'exp')), may hold values from 0 to 15, all different within a row; in each aligned block of 128 rows (0 to 127, 128 to 255, ...) at most 80 rows name the same one
- gate_fixed: int32 [4096, 8], P(('grp', 'exp')), may hold values from 1 to 65535
- w_gate: bfloat16 [16, 4096, 768], P('exp', None, 'grp'), may hold values from -0.09375 to 0.09375
- w_up: bfloat16 [16, 4096, 768], P('exp', None, 'grp'), may hold values from -0.09375 to 0.09375
- w_down: bfloat16 [16, 768, 4096], P('exp', 'grp'), may hold values from -0.21875 to 0.21875
Outputs:
- mixed: bfloat16 [4096, 4096], P(('grp', 'exp'))
The draws below stay inside these ranges and needn't reach their ends.
Inputs may be any that keep to these rules, and one draw needn't show every extreme that they name: `expert_ids`: each row names 8 different experts. Among the rows of one device no expert is named by more than 80 rows, and in every draw some expert is named by exactly 80 rows of some device.
All inputs are finite; a program needn't handle non-finite values.
Results may differ from the reference program's by a relative error of at most 0.0058.
Values may be sent and summed in bfloat16 or wider, within the bound.
A program may use at most 128 MiB of HBM per device.

```python
import math
import jax
import jax.numpy as jnp
import numpy as np
from jax import lax

D = 4096
FF = 768
EXPERTS = 16
TOPK = 8
TOK_DEV = 128
CAP = 80
TOKENS = 4096
DEVICES = 32


def touch_ends(values, stream_key, low, top_value):
    shape = values.shape
    index_at = [jax.random.randint(jax.random.fold_in(stream_key, axis), (), 0, shape[axis]) for axis in range(len(shape))]
    values = values.at[tuple(index_at)].set(low)
    longest = shape.index(max(shape))
    index_at[longest] = (index_at[longest] + 1) % shape[longest]
    return values.at[tuple(index_at)].set(top_value)


def steps_of(key, shape, cuts, low, high):
    def one(position, blocks):
        draws = jax.random.uniform(jax.random.fold_in(jax.random.fold_in(key, 6), position), (blocks,), jnp.float32, low / len(cuts), high / len(cuts))
        return jnp.repeat(jnp.exp(draws), shape[position] // blocks).reshape((-1,) + (1,) * (len(shape) - position - 1))

    factor_of = one(*cuts[0])
    for cut in cuts[1:]:
        factor_of = factor_of * one(*cut)
    return factor_of


def shared_out(own_key, own, number, rows, number_of, top, limit, lean):
    order = jax.random.permutation(own_key, number_of)
    crowded, ordinary = portions_of(number_of, rows * top, limit, lean, True), portions_of(number_of, rows * top, limit, lean, False)
    places = jnp.arange(number_of)

    def named(tallies, rotation):
        used = int((tallies > 0).sum())
        fixed = max(1, used // 4)
        passed = fixed + (places - fixed + rotation * (used - fixed)) % max(1, number_of - fixed)
        return jnp.zeros((number_of,), jnp.int32).at[order[jnp.where(places < fixed, places, passed)]].set(jnp.asarray(tallies, jnp.int32))

    tallies = jnp.where(number % 4 == 0, named(crowded, number // 4), named(ordinary, number - number // 4 - 1))
    mixed = jax.random.permutation(jax.random.fold_in(own, 3), number_of)
    giver, receiver = mixed[0:number_of // 2 * 2:2], mixed[1:number_of // 2 * 2:2]
    slack = jnp.minimum(tallies[giver] - 1, limit - tallies[receiver]) // 2
    slack = jnp.where((giver == order[0]) | (receiver == order[0]) | (tallies[receiver] == 0), 0, jnp.maximum(slack, 0))
    passed = jax.random.randint(jax.random.fold_in(own, 4), (number_of // 2,), 0, 1 << 20) % (slack + 1)
    tallies = tallies.at[giver].add(-passed).at[receiver].add(passed)
    members = jnp.searchsorted(jnp.cumsum(tallies), jnp.arange(rows * top), side="right").astype(jnp.int32)
    table = members.reshape(top, rows).T
    table = table[jax.random.permutation(jax.random.fold_in(own, 1), rows)]
    rotation = jax.random.randint(jax.random.fold_in(own, 2), (rows, 1), 0, top)
    return jnp.take_along_axis(table, (jnp.arange(top)[None, :] + rotation) % top, axis=1)


def portions_of(count, total, reach, skew, full):
    loads = [(1 << 20) // math.isqrt(rank ** skew) + 1 for rank in range(1, count + 1)]
    largest = reach if full else min(reach, max(-(-total // count), total * loads[0] // sum(loads)))
    least = 1 if total - largest >= count - 1 else 0
    given, rest = [largest] + [least] * (count - 1), total - largest - least * (count - 1)
    while rest > 0:
        candidates = [i for i in range(1, count) if given[i] < largest] or [i for i in range(1, count) if given[i] < reach]
        mass, left = sum([loads[i] for i in candidates]), rest
        for i in candidates:
            extra = min(reach - given[i], max(1, left * loads[i] // mass), rest)
            given[i] = given[i] + extra
            rest = rest - extra
    return np.array(given)


def scatter_about(stream_key, shape, deviation, most, cuts=(), kind=jnp.bfloat16):
    result = deviation * jax.random.normal(stream_key, shape, jnp.float32)
    if cuts:
        result = result * steps_of(stream_key, shape, cuts, -0.22, 0.18)
    return jnp.clip(result, -most, most).astype(kind)


def setup_inputs(seed: int = 0) -> dict:
    splits = jax.random.split(jax.random.key(seed), 7)
    tokens = scatter_about(splits[0], (TOKENS, D), 1.0, 6.0, ((0, 32),))
    expert_ids_keys = jax.random.split(jax.random.fold_in(splits[1], 1), TOKENS // TOK_DEV)
    expert_ids_turns = jax.random.permutation(jax.random.fold_in(splits[1], 3), TOKENS // TOK_DEV)
    expert_ids = jax.vmap(lambda own, number: shared_out(jax.random.fold_in(splits[1], 2), own, number, TOK_DEV, EXPERTS, TOPK, CAP, 2))(expert_ids_keys, expert_ids_turns).reshape((TOKENS, TOPK))
    gate_fixed = touch_ends(jax.random.randint(splits[2], (TOKENS, TOPK), 1, 65536), jax.random.fold_in(splits[2], 1), 1, 65535).astype(jnp.int32)
    w_gate = scatter_about(splits[3], (EXPERTS, D, FF), D ** -0.5, 0.09375, ((0, 8), (2, 4)))
    w_up = scatter_about(splits[4], (EXPERTS, D, FF), D ** -0.5, 0.09375, ((0, 8), (2, 4)))
    w_down = scatter_about(splits[5], (EXPERTS, FF, D), FF ** -0.5, 0.21875, ((0, 8), (1, 4)))
    return {"tokens": tokens, "expert_ids": expert_ids, "gate_fixed": gate_fixed, "w_gate": w_gate, "w_up": w_up, "w_down": w_down}


def reference(tokens, expert_ids, gate_fixed, w_gate, w_up, w_down):
    most_rows = DEVICES * CAP
    weight = gate_fixed.astype(jnp.float32) / 65536.0

    def one_expert(total, expert):
        chosen = expert_ids == expert
        routed = jnp.any(chosen, axis=1)
        order = jnp.argsort((1 - routed.astype(jnp.int32)), stable=True).astype(jnp.int32)
        picked = order[:most_rows]
        rows = tokens[picked]
        gate_part = jnp.dot(rows, w_gate[expert], preferred_element_type=jnp.float32)
        up_part = jnp.dot(rows, w_up[expert], preferred_element_type=jnp.float32)
        hidden = (jax.nn.silu(gate_part) * up_part).astype(jnp.bfloat16)
        expert_out = jnp.dot(hidden, w_down[expert], preferred_element_type=jnp.float32).astype(jnp.bfloat16)
        token_weight = jnp.sum(jnp.where(chosen, weight, 0.0), axis=1)[picked]
        term = token_weight[:, None] * expert_out.astype(jnp.float32)
        return total.at[picked].add(term), None

    start = jnp.zeros(tokens.shape, jnp.float32)
    total, unused = lax.scan(one_expert, start, jnp.arange(EXPERTS, dtype=jnp.int32))
    return total.astype(jnp.bfloat16)
```

```python
import jax
import jax.numpy as jnp
from jax import lax
from jax.sharding import Mesh
from jax.sharding import PartitionSpec as P

EXPERTS = 16


def per_device(tokens, expert_ids, gate_fixed, w_gate, w_up, w_down):
    local = w_gate.shape[0]
    onehot = expert_ids[:, :, None] == jnp.arange(EXPERTS, dtype=jnp.int32)[None, None, :]
    weight = jnp.sum(
        jnp.where(onehot, gate_fixed[:, :, None].astype(jnp.float32) / 65536.0, 0.0), axis=1
    )
    all_tokens = lax.all_gather(tokens, ("exp", "x"), axis=0, tiled=True)
    all_weight = lax.all_gather(weight, ("exp", "x"), axis=0, tiled=True)
    gate = lax.all_gather(w_gate, "core", axis=2, tiled=True)
    up = lax.all_gather(w_up, "core", axis=2, tiled=True)
    down = lax.all_gather(w_down, "core", axis=1, tiled=True)
    mine = lax.dynamic_slice_in_dim(all_weight, lax.axis_index("exp") * local, local, axis=1)
    total = None
    for one in range(local):
        gate_part = jnp.dot(all_tokens, gate[one], preferred_element_type=jnp.float32)
        up_part = jnp.dot(all_tokens, up[one], preferred_element_type=jnp.float32)
        hidden = (jax.nn.silu(gate_part) * up_part).astype(jnp.bfloat16)
        done = jnp.dot(hidden, down[one], preferred_element_type=jnp.float32)
        term = mine[:, one : one + 1] * done
        total = term if total is None else total + term
    part = lax.psum_scatter(
        total.astype(jnp.bfloat16), "exp", scatter_dimension=0, tiled=True
    )
    return lax.psum_scatter(part, "x", scatter_dimension=0, tiled=True)


def solution(mesh):
    grp, exp = mesh.shape["grp"], mesh.shape["exp"]
    split = Mesh(mesh.devices.reshape(grp // 2, 2, exp), ("x", "core", "exp"))
    rows = P(("x", "core", "exp"), None)
    in_specs = (
        rows,
        rows,
        rows,
        P("exp", None, ("x", "core")),
        P("exp", None, ("x", "core")),
        P("exp", ("x", "core"), None),
    )
    return jax.shard_map(
        per_device, mesh=split, in_specs=in_specs, out_specs=rows, check_vma=False
    )
```

```python
import jax
import jax.numpy as jnp
from jax import lax
from jax.sharding import Mesh
from jax.sharding import PartitionSpec as P

EXPERTS = 16


def per_device(tokens, expert_ids, gate_fixed, w_gate, w_up, w_down):
    local = w_gate.shape[0]
    onehot = expert_ids[:, :, None] == jnp.arange(EXPERTS, dtype=jnp.int32)[None, None, :]
    weight = jnp.sum(
        jnp.where(onehot, gate_fixed[:, :, None].astype(jnp.float32) / 65536.0, 0.0), axis=1
    )
    chips = lax.axis_size("x")
    blocks, axes = [(w_gate, w_up, w_down)], ("x", "core")
    if chips == 2:
        swap, axes = [(0, 1), (1, 0)], ("core",)
        blocks.append(tuple(lax.ppermute(panel, "x", swap) for panel in blocks[0]))
    all_tokens = lax.all_gather(tokens, "exp", axis=0, tiled=True)
    all_weight = lax.all_gather(weight, "exp", axis=0, tiled=True)
    mine = lax.dynamic_slice_in_dim(all_weight, lax.axis_index("exp") * local, local, axis=1)
    total = None
    for w_gate, w_up, w_down in blocks:
        gate = lax.all_gather(w_gate, axes, axis=2, tiled=True)
        up = lax.all_gather(w_up, axes, axis=2, tiled=True)
        down = lax.all_gather(w_down, axes, axis=1, tiled=True)
        for one in range(local):
            gate_part = jnp.dot(all_tokens, gate[one], preferred_element_type=jnp.float32)
            up_part = jnp.dot(all_tokens, up[one], preferred_element_type=jnp.float32)
            hidden = (jax.nn.silu(gate_part) * up_part).astype(jnp.bfloat16)
            done = jnp.dot(hidden, down[one], preferred_element_type=jnp.float32)
            term = mine[:, one : one + 1] * done
            total = term if total is None else total + term
    return lax.psum_scatter(
        total.astype(jnp.bfloat16), "exp", scatter_dimension=0, tiled=True
    )


def solution(mesh):
    grp, exp = mesh.shape["grp"], mesh.shape["exp"]
    split = Mesh(mesh.devices.reshape(grp // 2, 2, exp), ("x", "core", "exp"))
    rows = P(("x", "core", "exp"), None)
    in_specs = (
        rows,
        rows,
        rows,
        P("exp", None, ("x", "core")),
        P("exp", None, ("x", "core")),
        P("exp", ("x", "core"), None),
    )
    return jax.shard_map(
        per_device, mesh=split, in_specs=in_specs, out_specs=rows, check_vma=False
    )
```

```python
import jax
import jax.numpy as jnp
from jax import lax
from jax.sharding import Mesh
from jax.sharding import PartitionSpec as P

EXPERTS = 16


def per_device(tokens, expert_ids, gate_fixed, w_gate, w_up, w_down):
    local = w_gate.shape[0]
    onehot = expert_ids[:, :, None] == jnp.arange(EXPERTS, dtype=jnp.int32)[None, None, :]
    weight = jnp.sum(
        jnp.where(onehot, gate_fixed[:, :, None].astype(jnp.float32) / 65536.0, 0.0), axis=1
    )
    chips = lax.axis_size("x")
    blocks, axes = [(w_gate, w_up, w_down)], ("x", "core")
    if chips == 2:
        swap, axes = [(0, 1), (1, 0)], ("core",)
        blocks.append(tuple(lax.ppermute(panel, "x", swap) for panel in blocks[0]))
    all_tokens = lax.all_gather(tokens, "exp", axis=0, tiled=True)
    all_weight = lax.all_gather(weight, "exp", axis=0, tiled=True)
    mine = lax.dynamic_slice_in_dim(all_weight, lax.axis_index("exp") * local, local, axis=1)
    total = None
    for w_gate, w_up, w_down in blocks:
        gate = lax.all_gather(w_gate, axes, axis=2, tiled=True)
        up = lax.all_gather(w_up, axes, axis=2, tiled=True)
        down = lax.all_gather(w_down, axes, axis=1, tiled=True)
        hidden = []
        for one in range(local):
            gate_part = jnp.dot(all_tokens, gate[one], preferred_element_type=jnp.float32)
            up_part = jnp.dot(all_tokens, up[one], preferred_element_type=jnp.float32)
            value = jax.nn.silu(gate_part) * up_part * mine[:, one : one + 1]
            hidden.append(value.astype(jnp.bfloat16))
        term = jnp.dot(
            jnp.concatenate(hidden, axis=1),
            down.reshape(-1, down.shape[2]),
            preferred_element_type=jnp.float32,
        )
        total = term if total is None else total + term
    return lax.psum_scatter(
        total.astype(jnp.bfloat16), "exp", scatter_dimension=0, tiled=True
    )


def solution(mesh):
    grp, exp = mesh.shape["grp"], mesh.shape["exp"]
    split = Mesh(mesh.devices.reshape(grp // 2, 2, exp), ("x", "core", "exp"))
    rows = P(("x", "core", "exp"), None)
    in_specs = (
        rows,
        rows,
        rows,
        P("exp", None, ("x", "core")),
        P("exp", None, ("x", "core")),
        P("exp", ("x", "core"), None),
    )
    return jax.shard_map(
        per_device, mesh=split, in_specs=in_specs, out_specs=rows, check_vma=False
    )
```

```python
import jax
import jax.numpy as jnp
from jax import lax
from jax.sharding import Mesh
from jax.sharding import PartitionSpec as P

EXPERTS = 16


def per_device(tokens, expert_ids, gate_fixed, w_gate, w_up, w_down):
    local = w_gate.shape[0]
    onehot = expert_ids[:, :, None] == jnp.arange(EXPERTS, dtype=jnp.int32)[None, None, :]
    weight = jnp.sum(
        jnp.where(onehot, gate_fixed[:, :, None].astype(jnp.float32) / 65536.0, 0.0), axis=1
    )
    chips = lax.axis_size("x")
    blocks, axes = [(w_gate, w_up, w_down)], ("x", "core")
    if chips == 2:
        swap, axes = [(0, 1), (1, 0)], ("core",)
        blocks.append(tuple(lax.ppermute(panel, "x", swap) for panel in blocks[0]))
    all_tokens = lax.all_gather(tokens, "exp", axis=0, tiled=True)
    all_weight = lax.all_gather(weight, "exp", axis=0, tiled=True)
    mine = lax.dynamic_slice_in_dim(all_weight, lax.axis_index("exp") * local, local, axis=1)
    pairs = []
    for w_gate, w_up, w_down in blocks:
        gate = lax.all_gather(w_gate, axes, axis=2, tiled=True)
        up = lax.all_gather(w_up, axes, axis=2, tiled=True)
        down = lax.all_gather(w_down, axes, axis=1, tiled=True)
        hidden = []
        for one in range(local):
            gate_part = jnp.dot(all_tokens, gate[one], preferred_element_type=jnp.float32)
            up_part = jnp.dot(all_tokens, up[one], preferred_element_type=jnp.float32)
            value = jax.nn.silu(gate_part) * up_part * mine[:, one : one + 1]
            hidden.append(value.astype(jnp.bfloat16))
        pairs.append((jnp.concatenate(hidden, axis=1), down.reshape(-1, down.shape[2])))
    half = tokens.shape[1] // 2
    outputs = []
    for low in (0, half):
        total = None
        for hidden, down in pairs:
            term = jnp.dot(
                hidden, down[:, low : low + half], preferred_element_type=jnp.float32
            )
            total = term if total is None else total + term
        outputs.append(
            lax.psum_scatter(
                total.astype(jnp.bfloat16), "exp", scatter_dimension=0, tiled=True
            )
        )
    return jnp.concatenate(outputs, axis=1)


def solution(mesh):
    grp, exp = mesh.shape["grp"], mesh.shape["exp"]
    split = Mesh(mesh.devices.reshape(grp // 2, 2, exp), ("x", "core", "exp"))
    rows = P(("x", "core", "exp"), None)
    in_specs = (
        rows,
        rows,
        rows,
        P("exp", None, ("x", "core")),
        P("exp", None, ("x", "core")),
        P("exp", ("x", "core"), None),
    )
    return jax.shard_map(
        per_device, mesh=split, in_specs=in_specs, out_specs=rows, check_vma=False
    )
```
